32 devices in a mesh: groups: 2 (over y), rows: 4 (over z), cols: 2 (over x), chan: 2 (over core).
Axes of the slice: x: 2, y: 2, z: 4, core: 2. Of those that a mesh axis runs over, the one named last changes fastest.
Arguments:
- patches: bfloat16 [128, 16, 1024], P(('groups', 'rows'), 'cols', 'chan'), parts along dimension 0, may hold values from -6 to 6
- steps: float32 [128, 16, 1024], P(('groups', 'rows'), 'cols', 'chan'), parts along dimension 0, may hold values from 0.1 to 1
- decay_codes: int32 [128, 16], P(('groups', 'rows'), 'cols'), parts along dimension 0, may hold values from 0 to 15
- tissue_mask: int32 [128, 16], P(('groups', 'rows'), 'cols'), parts along dimension 0, may hold values 0 or 1
- decay_rates: float32 [16, 1024], P(None, 'chan'), may hold values from 0.002 to 4
- input_map: float32 [128, 16, 16], P(('groups', 'rows'), 'cols'), parts along dimension 0, may hold values from -1.5 to 1.5
- output_map: float32 [128, 16, 16], P(('groups', 'rows'), 'cols'), parts along dimension 0, may hold values from -1.5 to 1.5
- out_grad: bfloat16 [128, 16, 1024], P(('groups', 'rows'), 'cols', 'chan'), parts along dimension 0, may hold values from -0.59765625 to 0.59765625
Outputs:
- patches_grad: bfloat16 [128, 16, 1024], P(('groups', 'rows'), 'cols', 'chan'), parts along dimension 0
- steps_grad: float32 [128, 16, 1024], P(('groups', 'rows'), 'cols', 'chan'), parts along dimension 0
- input_map_grad: float32 [128, 16, 16], P(('groups', 'rows'), 'cols'), parts along dimension 0
- output_map_grad: float32 [128, 16, 16], P(('groups', 'rows'), 'cols'), parts along dimension 0
The draws below stay inside these ranges and needn't reach their ends.
There are 2 independent parts, one for each index of `groups`. The reference program is written for one: setup_inputs(seed, part) draws one part's arguments, and reference() takes and returns one part's arrays. A program takes and returns all parts, laid end to end along the dimension named above; an argument that names none is the same for every part. Nothing has to cross between parts.
Inputs may be any that keep to these rules, and one draw needn't show every extreme that they name: `decay_codes`: a decay code of each patch.
All inputs are finite; a program needn't handle non-finite values. No bound on the sum of `tissue_mask` on one device may be relied on, other than what follows from the above.
Results may differ from the reference program's by a relative error of at most 0.0014.
Values sent between devices are 32-bit elements; how exact they have to be, the bound alone decides.
A program may use at most 128 MiB of HBM per device.

```python
import math
import jax
import jax.numpy as jnp
from jax import lax

D = 1024
STATES = 16
CODES = 16
NR = 64
NC = 16


def place_ends(result, key, low, top_value):
    index_at = [jax.random.randint(jax.random.fold_in(key, axis), (), 0, length) for axis, length in enumerate(result.shape)]
    widest = result.shape.index(max(result.shape))
    next_to = index_at[:widest] + [(index_at[widest] + 1) % result.shape[widest]] + index_at[widest + 1:]
    return result.at[tuple(index_at)].set(low).at[tuple(next_to)].set(top_value)


def steps_of(own_key, shape, cuts, least, largest):
    gain = 1.0
    for position, blocks in cuts:
        draws = jax.random.uniform(jax.random.fold_in(jax.random.fold_in(own_key, 6), position), (blocks,), jnp.float32, least / len(cuts), largest / len(cuts))
        gain = gain * jnp.repeat(jnp.exp(draws), shape[position] // blocks).reshape((-1,) + (1,) * (len(shape) - 1 - position))
    return gain


def normal_values(stream_key, shape, scale, reach, cuts=(), dtype=jnp.bfloat16):
    result = jax.random.normal(stream_key, shape, jnp.float32) * scale
    if len(cuts) > 0:
        result = steps_of(stream_key, shape, cuts, -0.22, 0.18) * result
    return jnp.clip(result, min=-reach, max=reach).astype(dtype)


def setup_inputs(seed: int = 0, part: int = 0) -> dict:
    key_of = jax.random.split(jax.random.key(seed), 9)
    part_splits = jax.random.split(jax.random.fold_in(key_of[8], part), 9)
    patches = normal_values(part_splits[0], (NR, NC, D), 1.0, 6.0, ((0, 4), (1, 2), (2, 2)))
    steps = jnp.clip(jnp.exp(math.log(1.0) - 2.3025851 * jax.random.uniform(part_splits[1], (NR, NC, D), jnp.float32) ** steps_of(part_splits[1], (NR, NC, D), ((0, 4), (1, 2), (2, 2)), -0.2, 0.2)), 0.1, 1.0)
    decay_codes = place_ends(jax.random.randint(part_splits[2], (NR, NC), 0, CODES), jax.random.fold_in(part_splits[2], 1), 0, CODES - 1).astype(jnp.int32)
    tissue_mask = place_ends((jax.random.randint(part_splits[3], (NR, NC), 0, 4) < 3).astype(jnp.int32), jax.random.fold_in(part_splits[3], 1), 0, 1)
    decay_rates = jnp.clip(jnp.exp(math.log(4.0) - 7.6009024 * jax.random.uniform(key_of[4], (STATES, D), jnp.float32) ** steps_of(key_of[4], (STATES, D), ((1, 2),), -0.2, 0.2)), 0.002, 4.0)
    input_map = normal_values(part_splits[5], (NR, NC, STATES), 0.25, 1.5, ((0, 4), (1, 2)), jnp.float32)
    output_map = normal_values(part_splits[6], (NR, NC, STATES), 0.25, 1.5, ((0, 4), (1, 2)), jnp.float32)
    out_grad = normal_values(part_splits[7], (NR, NC, D), 0.1, 0.59765625, ((0, 4), (1, 2), (2, 2)))
    return {"patches": patches, "steps": steps, "decay_codes": decay_codes, "tissue_mask": tissue_mask, "decay_rates": decay_rates, "input_map": input_map, "output_map": output_map, "out_grad": out_grad}


def pair_combine(first, second):
    return (first[0] * second[0], second[0] * first[1] + second[1])


def block_grads(patches, steps, keep, maskf, rates, input_map, output_map, out_grad):
    xf = patches.astype(jnp.float32)
    gyf = out_grad.astype(jnp.float32)
    decay = jnp.exp(keep[:, :, None, None] * rates[None, None] * steps[:, :, None, :])
    drive = maskf[:, :, None] * steps * xf
    source = input_map[:, :, :, None] * drive[:, :, None, :]
    _, row_state = lax.associative_scan(pair_combine, (decay, source), axis=1)
    _, state = lax.associative_scan(pair_combine, (decay, row_state), axis=0)
    state_cot = output_map[:, :, :, None] * gyf[:, :, None, :]
    below = jnp.concatenate([decay[1:], jnp.ones_like(decay[:1])], axis=0)
    _, col_cot = lax.associative_scan(pair_combine, (below, state_cot), axis=0, reverse=True)
    right = jnp.concatenate([decay[:, 1:], jnp.ones_like(decay[:, :1])], axis=1)
    _, row_cot = lax.associative_scan(pair_combine, (right, col_cot), axis=1, reverse=True)
    above_state = jnp.concatenate([jnp.zeros_like(state[:1]), state[:-1]], axis=0)
    left_state = jnp.concatenate([jnp.zeros_like(row_state[:, :1]), row_state[:, :-1]], axis=1)
    decay_cot = decay * (col_cot * above_state + row_cot * left_state)
    drive_cot = jnp.sum(row_cot * input_map[:, :, :, None], axis=2)
    patches_grad = (drive_cot * maskf[:, :, None] * steps).astype(jnp.bfloat16)
    steps_grad = drive_cot * maskf[:, :, None] * xf + jnp.sum(decay_cot * keep[:, :, None, None] * rates[None, None], axis=2)
    map_in = jnp.sum(row_cot * drive[:, :, None, :], axis=3)
    map_out = jnp.sum(gyf[:, :, None, :] * state, axis=3)
    return patches_grad, steps_grad, map_in, map_out


def reference(patches, steps, decay_codes, tissue_mask, decay_rates, input_map, output_map, out_grad):
    maskf = tissue_mask.astype(jnp.float32)
    levels = 0.7 + 0.25 * decay_codes.astype(jnp.float32) / (CODES - 1)
    keep = maskf * jnp.log(levels)
    width = math.gcd(D, 128)
    count = D // width

    def split(field):
        return jnp.moveaxis(field.reshape(NR, NC, count, width), 2, 0)

    rate_blocks = jnp.moveaxis(decay_rates.reshape(STATES, count, width), 1, 0)

    def one_block(carry, pieces):
        xb, sb, rb, gb = pieces
        pg, sg, mi, mo = block_grads(xb, sb, keep, maskf, rb, input_map, output_map, gb)
        return (carry[0] + mi, carry[1] + mo), (pg, sg)

    zeros = jnp.zeros((NR, NC, STATES), jnp.float32)
    sums, grads = lax.scan(one_block, (zeros, zeros), (split(patches), split(steps), rate_blocks, split(out_grad)))

    def join(blocks):
        return jnp.moveaxis(blocks, 0, 2).reshape(NR, NC, D)

    return join(grads[0]), join(grads[1]), sums[0], sums[1]
```

```python
import functools

import jax
import jax.numpy as jnp
from jax import lax
from jax.experimental import pallas as pl
from jax.experimental.pallas import tpu as pltpu
from jax.sharding import PartitionSpec as P

CODES = 16
LANES = 128
F32 = jnp.float32
RIGHT, DOWN, UP, LEFT = range(4)


def kernel(dims, x_ref, steps_ref, codes_ref, mask_ref, rates_ref, imap_ref, omap_ref, gy_ref,
           gx_ref, gs_ref, sums_ref,
           im, om, kb, mb, lt, dr, gy, cs, decay, rst, cct,
           right_off, left_in, down_off, top_in, up_off, bottom_in, left_off, right_in,
           acc_in, acc_out, dc_rows, ds_rows, mine, theirs,
           send_sem, recv_sem, pair_send, pair_recv):
    rows, cols, chans, ni, nj, ns, chunks = dims
    row, col, chan = lax.axis_index("rows"), lax.axis_index("cols"), lax.axis_index("chan")
    peer = lax.rem(chan + 1, chans)
    first_row, last_row = row == 0, row == rows - 1
    first_col, last_col = col == 0, col == cols - 1

    barrier = pltpu.get_barrier_semaphore()

    def greet(there, target):
        @pl.when(there)
        def _():
            pl.semaphore_signal(barrier, inc=1, device_id=target, device_id_type=pl.DeviceIdType.MESH)

    greet(jnp.logical_not(first_row), {"rows": row - 1})
    greet(jnp.logical_not(last_row), {"rows": row + 1})
    greet(jnp.logical_not(first_col), {"cols": col - 1})
    greet(jnp.logical_not(last_col), {"cols": col + 1})
    pl.semaphore_signal(barrier, inc=1, device_id={"chan": peer}, device_id_type=pl.DeviceIdType.MESH)

    patches = ni * nj

    def turned(value, size):
        one = (lax.broadcasted_iota(jnp.int32, (size, size), 0)
               == lax.broadcasted_iota(jnp.int32, (size, size), 1)).astype(F32)
        return lax.dot_general(one, value, (((1,), (1,)), ((), ())),
                               precision=lax.Precision.HIGHEST, preferred_element_type=F32)

    maskf = mask_ref[...].astype(F32)
    keep = maskf * jnp.log(0.7 + 0.25 * codes_ref[...].astype(F32) / (CODES - 1))
    keep_t, mask_t = turned(keep, nj), turned(maskf, nj)
    for i in range(ni):
        kb[i] = jnp.broadcast_to(keep_t[:, i:i + 1], (nj, LANES))
        mb[i] = jnp.broadcast_to(mask_t[:, i:i + 1], (nj, LANES))
    im_t, om_t = turned(imap_ref[...], ns), turned(omap_ref[...], ns)
    for p in range(patches):
        im[p // nj, p % nj] = jnp.broadcast_to(im_t[:, p:p + 1], (ns, LANES))
        om[p // nj, p % nj] = jnp.broadcast_to(om_t[:, p:p + 1], (ns, LANES))

    @pl.when(first_col)
    def _():
        left_in[...] = jnp.zeros_like(left_in)

    @pl.when(last_col)
    def _():
        right_in[...] = jnp.zeros_like(right_in)

    @pl.when(first_row)
    def _():
        top_in[...] = jnp.zeros_like(top_in)

    @pl.when(last_row)
    def _():
        bottom_in[...] = jnp.zeros_like(bottom_in)

    def count(flag):
        return jnp.where(flag, 0, 1).astype(jnp.int32)

    pl.semaphore_wait(barrier, count(first_row) + count(last_row) + count(first_col) + count(last_col) + 1)

    def copy(kind, c):
        source, target, where = {
            RIGHT: (right_off, left_in, {"cols": col + 1}),
            LEFT: (left_off, right_in, {"cols": col - 1}),
            DOWN: (down_off, top_in, {"rows": row + 1}),
            UP: (up_off, bottom_in, {"rows": row - 1}),
        }[kind]
        return pltpu.make_async_remote_copy(
            src_ref=source.at[c], dst_ref=target.at[c],
            send_sem=send_sem.at[kind, c], recv_sem=recv_sem.at[kind, c],
            device_id=where, device_id_type=pl.DeviceIdType.MESH)

    source_edge = {RIGHT: first_col, LEFT: last_col, DOWN: first_row, UP: last_row}
    sink_edge = {RIGHT: last_col, LEFT: first_col, DOWN: last_row, UP: first_row}
    several = {RIGHT: cols > 1, LEFT: cols > 1, DOWN: rows > 1, UP: rows > 1}

    def send_first(kind, c):
        if several[kind]:
            @pl.when(source_edge[kind])
            def _():
                copy(kind, c).start()

    def lanes(c):
        return pl.ds(pl.multiple_of(c * LANES, LANES), LANES)

    def relay(kind, c):
        if not several[kind]:
            return
        inside = jnp.logical_not(jnp.logical_or(source_edge[kind], sink_edge[kind]))

        @pl.when(inside)
        def _():
            copy(kind, c).wait_recv()
            rates = rates_ref[:, lanes(c)]
            if kind in (DOWN, UP):
                off, entering = (down_off, top_in) if kind == DOWN else (up_off, bottom_in)
                for j in range(nj):
                    factor = jnp.exp(rates * cs[c, pl.ds(j, 1), :])
                    off[c, j] = factor * entering[c, j] + off[c, j]
            else:
                off, entering = (right_off, left_in) if kind == RIGHT else (left_off, right_in)

                @pl.loop(0, ni)
                def _(i):
                    factor = jnp.exp(rates * jnp.sum(lt[c, i], axis=0, keepdims=True))
                    off[c, i] = factor * entering[c, i] + off[c, i]
            copy(kind, c).start()

    def take_last(kind, c):
        if several[kind]:
            @pl.when(sink_edge[kind])
            def _():
                copy(kind, c).wait_recv()

    zero = jnp.zeros((ns, LANES), F32)

    def prepare(c):
        step = steps_ref[:, lanes(c)].reshape(ni, nj, LANES)
        logs = kb[...] * step
        lt[c] = logs
        cs[c] = jnp.sum(logs, axis=0)
        dr[c] = mb[...] * step * x_ref[:, lanes(c)].astype(F32).reshape(ni, nj, LANES)
        gy[c] = gy_ref[:, lanes(c)].astype(F32).reshape(ni, nj, LANES)

    def open_ends(c):
        rates = rates_ref[:, lanes(c)]

        def body(t, cot):
            i = ni - 1 - t
            r = zero
            cot = list(cot)
            for j in range(nj):
                a = jnp.exp(rates * lt[c, i, pl.ds(j, 1), :])
                decay[c, i, j] = a
                r = a * r + im[i, j] * dr[c, i, pl.ds(j, 1), :]
                cot[j] = a * (om[i, j] * gy[c, i, pl.ds(j, 1), :] + cot[j])
            right_off[c, i] = r
            return tuple(cot)

        cot = lax.fori_loop(0, ni, body, (zero,) * nj)
        for j in range(nj):
            up_off[c, j] = cot[j]

    def forward(c):
        def body(i, state):
            r = left_in[c, i]
            state = list(state)
            for j in range(nj):
                a = decay[c, i, j]
                r = a * r + im[i, j] * dr[c, i, pl.ds(j, 1), :]
                rst[c, i, j] = r
                state[j] = a * state[j] + r
            return tuple(state)

        state = lax.fori_loop(0, ni, body, (zero,) * nj)
        for j in range(nj):
            down_off[c, j] = state[j]

    def backward(c):
        def body(t, cot):
            i = ni - 1 - t
            lead = zero
            cot = list(cot)
            for j in reversed(range(nj)):
                a = decay[c, i, j]
                here = om[i, j] * gy[c, i, pl.ds(j, 1), :] + cot[j]
                cct[c, i, j] = here
                cot[j] = a * here
                lead = cot[j] + a * lead
            left_off[c, i] = lead
            return tuple(cot)

        lax.fori_loop(0, ni, body, tuple(bottom_in[c, j] for j in range(nj)))

    def gradients(c):
        rates = rates_ref[:, lanes(c)]

        def body(i, state):
            carry = right_in[c, i]
            state = list(state)
            for j in reversed(range(nj)):
                a, here, r = decay[c, i, j], cct[c, i, j], rst[c, i, j]
                before = rst[c, i, j - 1] if j else left_in[c, i]
                kept = a * state[j]
                state[j] = kept + r
                row_cot = here + carry
                carry = a * row_cot
                change = here * kept + carry * before
                acc_out[i, j] += gy[c, i, pl.ds(j, 1), :] * state[j]
                acc_in[i, j] += dr[c, i, pl.ds(j, 1), :] * row_cot
                dc_rows[i, pl.ds(j, 1), :] = jnp.sum(row_cot * im[i, j], axis=0, keepdims=True)
                ds_rows[i, pl.ds(j, 1), :] = jnp.sum(change * rates, axis=0, keepdims=True)
            return tuple(state)

        lax.fori_loop(0, ni, body, tuple(top_in[c, j] for j in range(nj)))
        step = steps_ref[:, lanes(c)].reshape(ni, nj, LANES)
        xf = x_ref[:, lanes(c)].astype(F32).reshape(ni, nj, LANES)
        drive_cot = dc_rows[...] * mb[...]
        gx_ref[:, lanes(c)] = (drive_cot * step).reshape(patches, LANES).astype(jnp.bfloat16)
        gs_ref[:, lanes(c)] = (drive_cot * xf + kb[...] * ds_rows[...]).reshape(patches, LANES)

    @pl.loop(0, chunks)
    def _(c):
        prepare(c)
        open_ends(c)
        send_first(RIGHT, c)
        send_first(UP, c)

    acc_in[...] = jnp.zeros_like(acc_in)
    acc_out[...] = jnp.zeros_like(acc_out)

    def do_forward(c):
        relay(RIGHT, c)
        take_last(RIGHT, c)
        forward(c)
        send_first(DOWN, c)

    def do_backward(c):
        relay(UP, c)
        take_last(UP, c)
        backward(c)
        send_first(LEFT, c)

    upper = row < rows // 2

    @pl.loop(0, chunks)
    def _(c):
        @pl.when(upper)
        def _():
            do_forward(c)
            do_backward(c)

        @pl.when(jnp.logical_not(upper))
        def _():
            do_backward(c)
            do_forward(c)

        @pl.when(c > 0)
        def _():
            relay(DOWN, c - 1)

    relay(DOWN, chunks - 1)

    @pl.loop(0, chunks)
    def _(c):
        take_last(DOWN, c)
        relay(LEFT, c)
        take_last(LEFT, c)
        gradients(c)

    ones = jnp.ones((8, LANES), F32)

    def lane_sums(acc):
        return lax.dot_general(ones, acc[...].reshape(patches * ns, LANES), (((1,), (1,)), ((), ())),
                               precision=lax.Precision.HIGHEST, preferred_element_type=F32)

    which = lax.broadcasted_iota(jnp.int32, (8, patches * ns), 0)
    mine[...] = jnp.where(which == 0, lane_sums(acc_in), lane_sums(acc_out))
    swap = pltpu.make_async_remote_copy(
        src_ref=mine, dst_ref=theirs, send_sem=pair_send, recv_sem=pair_recv,
        device_id={"chan": peer}, device_id_type=pl.DeviceIdType.MESH)
    swap.start()
    for kind in (RIGHT, UP, DOWN, LEFT):
        if several[kind]:
            @pl.when(jnp.logical_not(sink_edge[kind]))
            def _():
                @pl.loop(0, chunks)
                def _(c):
                    copy(kind, c).wait_send()
    swap.wait()
    sums_ref[...] = mine[...] + theirs[...]


def local(sizes, patches, steps, decay_codes, tissue_mask, decay_rates, input_map, output_map, out_grad):
    rows, cols, chans = sizes
    ni, nj, width = steps.shape
    ns = decay_rates.shape[0]
    chunks = width // LANES
    count = ni * nj
    vmem = pl.BlockSpec(memory_space=pltpu.VMEM)

    def buf(*shape):
        return pltpu.VMEM(shape, F32)

    across = buf(chunks, ni, ns, LANES)
    along = buf(chunks, nj, ns, LANES)
    whole = buf(chunks, ni, nj, ns, LANES)
    tile = buf(ni, nj, LANES)
    tiles = buf(chunks, ni, nj, LANES)
    maps = buf(ni, nj, ns, LANES)
    gx, gs, sums = pl.pallas_call(
        functools.partial(kernel, (rows, cols, chans, ni, nj, ns, chunks)),
        out_shape=(
            jax.ShapeDtypeStruct((count, width), jnp.bfloat16),
            jax.ShapeDtypeStruct((count, width), F32),
            jax.ShapeDtypeStruct((8, count * ns), F32),
        ),
        in_specs=[vmem] * 8,
        out_specs=(vmem,) * 3,
        scratch_shapes=[
            maps, maps, tile, tile, tiles, tiles, tiles, buf(chunks, nj, LANES), whole, whole, whole,
            across, across, along, along, along, along, across, across,
            maps, maps, tile, tile, buf(8, count * ns), buf(8, count * ns),
            pltpu.SemaphoreType.DMA((4, chunks)), pltpu.SemaphoreType.DMA((4, chunks)),
            pltpu.SemaphoreType.DMA, pltpu.SemaphoreType.DMA,
        ],
        compiler_params=pltpu.CompilerParams(
            collective_id=0, has_side_effects=True, vmem_limit_bytes=44 * 1024 * 1024),
        cost_estimate=pl.CostEstimate(
            flops=40 * count * ns * width, bytes_accessed=16 * count * width,
            transcendentals=count * ns * width),
    )(patches.reshape(count, width), steps.reshape(count, width), decay_codes, tissue_mask, decay_rates,
      input_map.reshape(count, ns), output_map.reshape(count, ns), out_grad.reshape(count, width))
    shape = (ni, nj, width)
    return (gx.reshape(shape), gs.reshape(shape),
            sums[0].reshape(ni, nj, ns), sums[1].reshape(ni, nj, ns))


def solution(mesh):
    field = P(("groups", "rows"), "cols", "chan")
    plain = P(("groups", "rows"), "cols")
    proj = P(("groups", "rows"), "cols", None)
    sizes = (mesh.shape["rows"], mesh.shape["cols"], mesh.shape["chan"])
    return jax.shard_map(
        functools.partial(local, sizes), mesh=mesh,
        in_specs=(field, field, plain, plain, P(None, "chan"), proj, proj, field),
        out_specs=(field, field, proj, proj), check_vma=False)
```

```python
import functools

import jax
import jax.numpy as jnp
from jax import lax
from jax.experimental import pallas as pl
from jax.experimental.pallas import tpu as pltpu
from jax.sharding import PartitionSpec as P

CODES = 16
LANES = 128
F32 = jnp.float32
RIGHT, DOWN, UP, LEFT = range(4)


def kernel(dims, x_hbm, steps_hbm, codes_hbm, mask_hbm, rates_hbm, imap_hbm, omap_hbm, gy_hbm,
           gx_ref, gs_ref, gi_ref, go_ref,
           x_ref, steps_ref, codes_ref, mask_ref, rates_ref, imap_ref, omap_ref, gy_ref, load_sem,
           im, om, kb, mb, lt, dr, gy, cs, decay, rst, cct,
           right_off, left_in, down_off, top_in, up_off, bottom_in, left_off, right_in,
           acc_in, acc_out, dc_rows, ds_rows, mine, theirs,
           send_sem, recv_sem, pair_send, pair_recv):
    rows, cols, chans, ni, nj, ns, chunks = dims
    row, col, chan = lax.axis_index("rows"), lax.axis_index("cols"), lax.axis_index("chan")
    peer = lax.rem(chan + 1, chans)
    first_row, last_row = row == 0, row == rows - 1
    first_col, last_col = col == 0, col == cols - 1

    loads = [pltpu.make_async_copy(source, target, load_sem.at[k]) for k, (source, target) in enumerate((
        (codes_hbm, codes_ref), (mask_hbm, mask_ref), (imap_hbm, imap_ref), (omap_hbm, omap_ref),
        (rates_hbm, rates_ref), (steps_hbm, steps_ref), (x_hbm, x_ref), (gy_hbm, gy_ref)))]
    for load in loads:
        load.start()

    barrier = pltpu.get_barrier_semaphore()

    def greet(there, target):
        @pl.when(there)
        def _():
            pl.semaphore_signal(barrier, inc=1, device_id=target, device_id_type=pl.DeviceIdType.MESH)

    greet(jnp.logical_not(first_row), {"rows": row - 1})
    greet(jnp.logical_not(last_row), {"rows": row + 1})
    greet(jnp.logical_not(first_col), {"cols": col - 1})
    greet(jnp.logical_not(last_col), {"cols": col + 1})
    pl.semaphore_signal(barrier, inc=1, device_id={"chan": peer}, device_id_type=pl.DeviceIdType.MESH)

    patches = ni * nj

    def turned(value, size):
        one = (lax.broadcasted_iota(jnp.int32, (size, size), 0)
               == lax.broadcasted_iota(jnp.int32, (size, size), 1)).astype(F32)
        return lax.dot_general(one, value, (((1,), (1,)), ((), ())),
                               precision=lax.Precision.HIGHEST, preferred_element_type=F32)

    for load in loads[:4]:
        load.wait()
    mask_t = mask_ref[...].astype(F32)
    keep_t = mask_t * jnp.log(0.7 + 0.25 * codes_ref[...].astype(F32) / (CODES - 1))
    for i in range(ni):
        kb[i] = jnp.broadcast_to(keep_t[:, i:i + 1], (nj, LANES))
        mb[i] = jnp.broadcast_to(mask_t[:, i:i + 1], (nj, LANES))
    im_t, om_t = turned(imap_ref[...], ns), turned(omap_ref[...], ns)
    for p in range(patches):
        im[p // nj, p % nj] = jnp.broadcast_to(im_t[:, p:p + 1], (ns, LANES))
        om[p // nj, p % nj] = jnp.broadcast_to(om_t[:, p:p + 1], (ns, LANES))

    for load in loads[4:]:
        load.wait()

    @pl.when(first_col)
    def _():
        left_in[...] = jnp.zeros_like(left_in)

    @pl.when(last_col)
    def _():
        right_in[...] = jnp.zeros_like(right_in)

    @pl.when(first_row)
    def _():
        top_in[...] = jnp.zeros_like(top_in)

    @pl.when(last_row)
    def _():
        bottom_in[...] = jnp.zeros_like(bottom_in)

    def count(flag):
        return jnp.where(flag, 0, 1).astype(jnp.int32)

    pl.semaphore_wait(barrier, count(first_row) + count(last_row) + count(first_col) + count(last_col) + 1)

    def copy(kind, c):
        source, target, where = {
            RIGHT: (right_off, left_in, {"cols": col + 1}),
            LEFT: (left_off, right_in, {"cols": col - 1}),
            DOWN: (down_off, top_in, {"rows": row + 1}),
            UP: (up_off, bottom_in, {"rows": row - 1}),
        }[kind]
        return pltpu.make_async_remote_copy(
            src_ref=source.at[c], dst_ref=target.at[c],
            send_sem=send_sem.at[kind, c], recv_sem=recv_sem.at[kind, c],
            device_id=where, device_id_type=pl.DeviceIdType.MESH)

    source_edge = {RIGHT: first_col, LEFT: last_col, DOWN: first_row, UP: last_row}
    sink_edge = {RIGHT: last_col, LEFT: first_col, DOWN: last_row, UP: first_row}
    several = {RIGHT: cols > 1, LEFT: cols > 1, DOWN: rows > 1, UP: rows > 1}

    def send_first(kind, c):
        if several[kind]:
            @pl.when(source_edge[kind])
            def _():
                copy(kind, c).start()

    def lanes(c):
        return pl.ds(pl.multiple_of(c * LANES, LANES), LANES)

    def relay(kind, c):
        if not several[kind]:
            return
        inside = jnp.logical_not(jnp.logical_or(source_edge[kind], sink_edge[kind]))

        @pl.when(inside)
        def _():
            copy(kind, c).wait_recv()
            rates = rates_ref[:, lanes(c)]
            if kind in (DOWN, UP):
                off, entering = (down_off, top_in) if kind == DOWN else (up_off, bottom_in)
                for j in range(nj):
                    factor = jnp.exp(rates * cs[c, pl.ds(j, 1), :])
                    off[c, j] = factor * entering[c, j] + off[c, j]
            else:
                off, entering = (right_off, left_in) if kind == RIGHT else (left_off, right_in)

                @pl.loop(0, ni)
                def _(i):
                    factor = jnp.exp(rates * jnp.sum(lt[c, i], axis=0, keepdims=True))
                    off[c, i] = factor * entering[c, i] + off[c, i]
            copy(kind, c).start()

    def take_last(kind, c):
        if several[kind]:
            @pl.when(sink_edge[kind])
            def _():
                copy(kind, c).wait_recv()

    zero = jnp.zeros((ns, LANES), F32)

    def prepare(c):
        step = steps_ref[:, lanes(c)].reshape(ni, nj, LANES)
        logs = kb[...] * step
        lt[c] = logs
        cs[c] = jnp.sum(logs, axis=0)
        dr[c] = mb[...] * step * x_ref[:, lanes(c)].astype(F32).reshape(ni, nj, LANES)
        gy[c] = gy_ref[:, lanes(c)].astype(F32).reshape(ni, nj, LANES)

    group = 2 if ni % 2 == 0 else 1

    def down_rows(body, carry):
        def several_rows(t, carry):
            for k in range(group):
                carry = body(t * group + k, carry)
            return carry

        return lax.fori_loop(0, ni // group, several_rows, carry)

    def up_rows(body, carry):
        return down_rows(lambda t, value: body(ni - 1 - t, value), carry)

    def open_ends(c):
        rates = rates_ref[:, lanes(c)]

        def body(i, cot):
            r = zero
            cot = list(cot)
            for j in range(nj):
                a = jnp.exp(rates * lt[c, i, pl.ds(j, 1), :])
                decay[c, i, j] = a
                r = a * r + im[i, j] * dr[c, i, pl.ds(j, 1), :]
                cot[j] = a * (om[i, j] * gy[c, i, pl.ds(j, 1), :] + cot[j])
            right_off[c, i] = r
            return tuple(cot)

        cot = up_rows(body, (zero,) * nj)
        for j in range(nj):
            up_off[c, j] = cot[j]

    def forward(c):
        def body(i, state):
            r = left_in[c, i]
            state = list(state)
            for j in range(nj):
                a = decay[c, i, j]
                r = a * r + im[i, j] * dr[c, i, pl.ds(j, 1), :]
                rst[c, i, j] = r
                state[j] = a * state[j] + r
            return tuple(state)

        state = down_rows(body, (zero,) * nj)
        for j in range(nj):
            down_off[c, j] = state[j]

    def backward(c):
        def body(i, cot):
            lead = zero
            cot = list(cot)
            for j in reversed(range(nj)):
                a = decay[c, i, j]
                here = om[i, j] * gy[c, i, pl.ds(j, 1), :] + cot[j]
                cct[c, i, j] = here
                cot[j] = a * here
                lead = cot[j] + a * lead
            left_off[c, i] = lead
            return tuple(cot)

        up_rows(body, tuple(bottom_in[c, j] for j in range(nj)))

    def gradients(c):
        rates = rates_ref[:, lanes(c)]

        def body(i, state):
            carry = right_in[c, i]
            state = list(state)
            for j in reversed(range(nj)):
                a, here, r = decay[c, i, j], cct[c, i, j], rst[c, i, j]
                before = rst[c, i, j - 1] if j else left_in[c, i]
                kept = a * state[j]
                state[j] = kept + r
                row_cot = here + carry
                carry = a * row_cot
                change = here * kept + carry * before
                acc_out[i, j] += gy[c, i, pl.ds(j, 1), :] * state[j]
                acc_in[i, j] += dr[c, i, pl.ds(j, 1), :] * row_cot
                dc_rows[i, pl.ds(j, 1), :] = jnp.sum(row_cot * im[i, j], axis=0, keepdims=True)
                ds_rows[i, pl.ds(j, 1), :] = jnp.sum(change * rates, axis=0, keepdims=True)
            return tuple(state)

        down_rows(body, tuple(top_in[c, j] for j in range(nj)))
        step = steps_ref[:, lanes(c)].reshape(ni, nj, LANES)
        xf = x_ref[:, lanes(c)].astype(F32).reshape(ni, nj, LANES)
        drive_cot = dc_rows[...] * mb[...]
        gx_ref[:, lanes(c)] = (drive_cot * step).reshape(patches, LANES).astype(jnp.bfloat16)
        gs_ref[:, lanes(c)] = (drive_cot * xf + kb[...] * ds_rows[...]).reshape(patches, LANES)

    @pl.loop(0, chunks)
    def _(c):
        prepare(c)
        open_ends(c)
        send_first(RIGHT, c)
        send_first(UP, c)

    acc_in[...] = jnp.zeros_like(acc_in)
    acc_out[...] = jnp.zeros_like(acc_out)

    def do_forward(c):
        relay(RIGHT, c)
        take_last(RIGHT, c)
        forward(c)
        send_first(DOWN, c)

    def do_backward(c):
        take_last(UP, c)
        backward(c)
        send_first(LEFT, c)

    upper = row < rows // 2

    @pl.loop(0, chunks)
    def _(c):
        relay(UP, c)

        @pl.when(upper)
        def _():
            do_forward(c)
            do_backward(c)

        @pl.when(jnp.logical_not(upper))
        def _():
            do_backward(c)
            do_forward(c)

        @pl.when(c > 0)
        def _():
            relay(DOWN, c - 1)

    relay(DOWN, chunks - 1)

    @pl.loop(0, chunks)
    def _(c):
        take_last(DOWN, c)
        relay(LEFT, c)
        take_last(LEFT, c)
        gradients(c)

    ones = jnp.ones((8, LANES), jnp.bfloat16)

    def lane_sums(acc):
        whole = acc[...].reshape(patches * ns, LANES)
        high = whole.astype(jnp.bfloat16)
        low = (whole - high.astype(F32)).astype(jnp.bfloat16)

        def dot(part):
            return lax.dot_general(ones, part, (((1,), (1,)), ((), ())), preferred_element_type=F32)

        return dot(high) + dot(low)

    for which, acc in enumerate((acc_in, acc_out)):
        flat = lane_sums(acc)
        for i in range(ni):
            mine[which, pl.ds(i, 1), :] = flat[0:1, i * nj * ns:(i + 1) * nj * ns]
    swap = pltpu.make_async_remote_copy(
        src_ref=mine, dst_ref=theirs, send_sem=pair_send, recv_sem=pair_recv,
        device_id={"chan": peer}, device_id_type=pl.DeviceIdType.MESH)
    swap.start()
    for kind in (RIGHT, UP, DOWN, LEFT):
        if several[kind]:
            @pl.when(jnp.logical_not(sink_edge[kind]))
            def _():
                @pl.loop(0, chunks)
                def _(c):
                    copy(kind, c).wait_send()
    swap.wait()
    for which, target in enumerate((gi_ref, go_ref)):
        total = mine[which] + theirs[which]
        for j in range(nj):
            target[:, j, :] = total[:, j * ns:(j + 1) * ns]


def finish(*refs):
    half = (len(refs) - 1) // 2
    sem = refs[-1]
    stores = [pltpu.make_async_copy(refs[k], refs[half + k], sem.at[k]) for k in range(half)]
    for store in stores:
        store.start()
    for store in stores:
        store.wait()


def local(sizes, patches, steps, decay_codes, tissue_mask, decay_rates, input_map, output_map, out_grad):
    rows, cols, chans = sizes
    ni, nj, width = steps.shape
    ns = decay_rates.shape[0]
    chunks = width // LANES
    count = ni * nj
    vmem = pl.BlockSpec(memory_space=pltpu.VMEM)
    hbm = pl.BlockSpec(memory_space=pltpu.HBM)

    def buf(*shape):
        return pltpu.VMEM(shape, F32)

    across = buf(chunks, ni, ns, LANES)
    along = buf(chunks, nj, ns, LANES)
    whole = buf(chunks, ni, nj, ns, LANES)
    tile = buf(ni, nj, LANES)
    tiles = buf(chunks, ni, nj, LANES)
    maps = buf(ni, nj, ns, LANES)
    results = pl.pallas_call(
        functools.partial(kernel, (rows, cols, chans, ni, nj, ns, chunks)),
        out_shape=(
            jax.ShapeDtypeStruct((count, width), jnp.bfloat16),
            jax.ShapeDtypeStruct((count, width), F32),
            jax.ShapeDtypeStruct((ni, nj, ns), F32),
            jax.ShapeDtypeStruct((ni, nj, ns), F32),
        ),
        in_specs=[hbm] * 8,
        out_specs=(vmem,) * 4,
        scratch_shapes=[
            pltpu.VMEM((count, width), jnp.bfloat16), buf(count, width), pltpu.VMEM((nj, ni), jnp.int32),
            pltpu.VMEM((nj, ni), jnp.int32), buf(ns, width), buf(count, ns), buf(count, ns),
            pltpu.VMEM((count, width), jnp.bfloat16), pltpu.SemaphoreType.DMA((8,)),
            maps, maps, tile, tile, tiles, tiles, tiles, buf(chunks, nj, LANES), whole, whole, whole,
            across, across, along, along, along, along, across, across,
            maps, maps, tile, tile, buf(2, ni, nj * ns), buf(2, ni, nj * ns),
            pltpu.SemaphoreType.DMA((4, chunks)), pltpu.SemaphoreType.DMA((4, chunks)),
            pltpu.SemaphoreType.DMA, pltpu.SemaphoreType.DMA,
        ],
        compiler_params=pltpu.CompilerParams(
            collective_id=0, has_side_effects=True, vmem_limit_bytes=63 * 1024 * 1024),
        cost_estimate=pl.CostEstimate(
            flops=40 * count * ns * width, bytes_accessed=16 * count * width,
            transcendentals=count * ns * width),
    )(patches.reshape(count, width), steps.reshape(count, width), decay_codes.T, tissue_mask.T, decay_rates,
      input_map.reshape(count, ns), output_map.reshape(count, ns), out_grad.reshape(count, width))
    gx, gs, gi, go = pl.pallas_call(
        finish,
        out_shape=tuple(jax.ShapeDtypeStruct(value.shape, value.dtype) for value in results),
        in_specs=[pl.BlockSpec(memory_space=pl.ANY)] * 4,
        out_specs=(hbm,) * 4,
        scratch_shapes=[pltpu.SemaphoreType.DMA((4,))],
    )(*results)
    shape = (ni, nj, width)
    return gx.reshape(shape), gs.reshape(shape), gi, go


def solution(mesh):
    field = P(("groups", "rows"), "cols", "chan")
    plain = P(("groups", "rows"), "cols")
    proj = P(("groups", "rows"), "cols", None)
    sizes = (mesh.shape["rows"], mesh.shape["cols"], mesh.shape["chan"])
    return jax.shard_map(
        functools.partial(local, sizes), mesh=mesh,
        in_specs=(field, field, plain, plain, P(None, "chan"), proj, proj, field),
        out_specs=(field, field, proj, proj), check_vma=False)
```

```python
import functools

import jax
import jax.numpy as jnp
from jax import lax
from jax.experimental import pallas as pl
from jax.experimental.pallas import tpu as pltpu
from jax.sharding import PartitionSpec as P

CODES = 16
LANES = 128
F32 = jnp.float32
RIGHT, DOWN, UP, LEFT = range(4)


def kernel(dims, x_hbm, steps_hbm, codes_hbm, mask_hbm, rates_hbm, imap_hbm, omap_hbm, gy_hbm,
           gx_ref, gs_ref, gi_ref, go_ref,
           x_ref, steps_ref, codes_ref, mask_ref, rates_ref, imap_ref, omap_ref, gy_ref, load_sem,
           im, om, kb, mb, lt, dr, gy, cs, decay, rst, cct,
           right_off, left_in, down_off, top_in, up_off, bottom_in, left_off, right_in,
           acc_in, acc_out, dc_rows, ds_rows, mine, theirs,
           send_sem, recv_sem, pair_send, pair_recv):
    rows, cols, chans, ni, nj, ns, chunks = dims
    row, col, chan = lax.axis_index("rows"), lax.axis_index("cols"), lax.axis_index("chan")
    peer = lax.rem(chan + 1, chans)
    first_row, last_row = row == 0, row == rows - 1
    first_col, last_col = col == 0, col == cols - 1

    loads = [pltpu.make_async_copy(source, target, load_sem.at[k]) for k, (source, target) in enumerate((
        (codes_hbm, codes_ref), (mask_hbm, mask_ref), (imap_hbm, imap_ref), (omap_hbm, omap_ref),
        (rates_hbm, rates_ref), (steps_hbm, steps_ref), (x_hbm, x_ref), (gy_hbm, gy_ref)))]
    for load in loads:
        load.start()

    barrier = pltpu.get_barrier_semaphore()

    def greet(there, target):
        @pl.when(there)
        def _():
            pl.semaphore_signal(barrier, inc=1, device_id=target, device_id_type=pl.DeviceIdType.MESH)

    greet(jnp.logical_not(first_row), {"rows": row - 1})
    greet(jnp.logical_not(last_row), {"rows": row + 1})
    greet(jnp.logical_not(first_col), {"cols": col - 1})
    greet(jnp.logical_not(last_col), {"cols": col + 1})
    pl.semaphore_signal(barrier, inc=1, device_id={"chan": peer}, device_id_type=pl.DeviceIdType.MESH)

    patches = ni * nj

    def turned(value, size):
        one = (lax.broadcasted_iota(jnp.int32, (size, size), 0)
               == lax.broadcasted_iota(jnp.int32, (size, size), 1)).astype(F32)
        return lax.dot_general(one, value, (((1,), (1,)), ((), ())),
                               precision=lax.Precision.HIGHEST, preferred_element_type=F32)

    for load in loads[:4]:
        load.wait()
    mask_t = mask_ref[...].astype(F32)
    keep_t = mask_t * jnp.log(0.7 + 0.25 * codes_ref[...].astype(F32) / (CODES - 1))
    for i in range(ni):
        kb[i] = jnp.broadcast_to(keep_t[:, i:i + 1], (nj, LANES))
        mb[i] = jnp.broadcast_to(mask_t[:, i:i + 1], (nj, LANES))
    im_t, om_t = turned(imap_ref[...], ns), turned(omap_ref[...], ns)
    for p in range(patches):
        im[p // nj, p % nj] = jnp.broadcast_to(im_t[:, p:p + 1], (ns, LANES))
        om[p // nj, p % nj] = jnp.broadcast_to(om_t[:, p:p + 1], (ns, LANES))

    for load in loads[4:]:
        load.wait()

    @pl.when(first_col)
    def _():
        left_in[...] = jnp.zeros_like(left_in)

    @pl.when(last_col)
    def _():
        right_in[...] = jnp.zeros_like(right_in)

    @pl.when(first_row)
    def _():
        top_in[...] = jnp.zeros_like(top_in)

    @pl.when(last_row)
    def _():
        bottom_in[...] = jnp.zeros_like(bottom_in)

    def count(flag):
        return jnp.where(flag, 0, 1).astype(jnp.int32)

    pl.semaphore_wait(barrier, count(first_row) + count(last_row) + count(first_col) + count(last_col) + 1)

    def copy(kind, c):
        source, target, where = {
            RIGHT: (right_off, left_in, {"cols": col + 1}),
            LEFT: (left_off, right_in, {"cols": col - 1}),
            DOWN: (down_off, top_in, {"rows": row + 1}),
            UP: (up_off, bottom_in, {"rows": row - 1}),
        }[kind]
        return pltpu.make_async_remote_copy(
            src_ref=source.at[c], dst_ref=target.at[c],
            send_sem=send_sem.at[kind, c], recv_sem=recv_sem.at[kind, c],
            device_id=where, device_id_type=pl.DeviceIdType.MESH)

    source_edge = {RIGHT: first_col, LEFT: last_col, DOWN: first_row, UP: last_row}
    sink_edge = {RIGHT: last_col, LEFT: first_col, DOWN: last_row, UP: first_row}
    several = {RIGHT: cols > 1, LEFT: cols > 1, DOWN: rows > 1, UP: rows > 1}

    def send_first(kind, c):
        if several[kind]:
            @pl.when(source_edge[kind])
            def _():
                copy(kind, c).start()

    def lanes(c):
        return pl.ds(pl.multiple_of(c * LANES, LANES), LANES)

    def relay(kind, c):
        if not several[kind]:
            return
        inside = jnp.logical_not(jnp.logical_or(source_edge[kind], sink_edge[kind]))

        @pl.when(inside)
        def _():
            copy(kind, c).wait_recv()
            rates = rates_ref[:, lanes(c)]
            if kind in (DOWN, UP):
                off, entering = (down_off, top_in) if kind == DOWN else (up_off, bottom_in)
                for j in range(nj):
                    factor = jnp.exp(rates * cs[c, pl.ds(j, 1), :])
                    off[c, j] = factor * entering[c, j] + off[c, j]
            else:
                off, entering = (right_off, left_in) if kind == RIGHT else (left_off, right_in)

                @pl.loop(0, ni)
                def _(i):
                    factor = jnp.exp(rates * jnp.sum(lt[c, i], axis=0, keepdims=True))
                    off[c, i] = factor * entering[c, i] + off[c, i]
            copy(kind, c).start()

    def take_last(kind, c):
        if several[kind]:
            @pl.when(sink_edge[kind])
            def _():
                copy(kind, c).wait_recv()

    zero = jnp.zeros((ns, LANES), F32)

    def prepare(c):
        step = steps_ref[:, lanes(c)].reshape(ni, nj, LANES)
        logs = kb[...] * step
        lt[c] = logs
        cs[c] = jnp.sum(logs, axis=0)
        dr[c] = mb[...] * step * x_ref[:, lanes(c)].astype(F32).reshape(ni, nj, LANES)
        gy[c] = gy_ref[:, lanes(c)].astype(F32).reshape(ni, nj, LANES)

    group = 2 if ni % 2 == 0 else 1

    def down_rows(body, carry):
        def several_rows(t, carry):
            for k in range(group):
                carry = body(t * group + k, carry)
            return carry

        return lax.fori_loop(0, ni // group, several_rows, carry)

    def up_rows(body, carry):
        return down_rows(lambda t, value: body(ni - 1 - t, value), carry)

    def open_ends(c):
        rates = rates_ref[:, lanes(c)]

        def body(i, cot):
            r = zero
            cot = list(cot)
            for j in range(nj):
                a = jnp.exp(rates * lt[c, i, pl.ds(j, 1), :])
                decay[c, i, j] = a
                r = a * r + im[i, j] * dr[c, i, pl.ds(j, 1), :]
                cot[j] = a * (om[i, j] * gy[c, i, pl.ds(j, 1), :] + cot[j])
            right_off[c, i] = r
            return tuple(cot)

        cot = up_rows(body, (zero,) * nj)
        for j in range(nj):
            up_off[c, j] = cot[j]

    def forward(c):
        def body(i, state):
            r = left_in[c, i]
            state = list(state)
            for j in range(nj):
                a = decay[c, i, j]
                r = a * r + im[i, j] * dr[c, i, pl.ds(j, 1), :]
                rst[c, i, j] = r
                state[j] = a * state[j] + r
            return tuple(state)

        state = down_rows(body, (zero,) * nj)
        for j in range(nj):
            down_off[c, j] = state[j]

    def backward(c):
        def body(i, cot):
            lead = zero
            cot = list(cot)
            for j in reversed(range(nj)):
                a = decay[c, i, j]
                here = om[i, j] * gy[c, i, pl.ds(j, 1), :] + cot[j]
                cct[c, i, j] = here
                cot[j] = a * here
                lead = cot[j] + a * lead
            left_off[c, i] = lead
            return tuple(cot)

        up_rows(body, tuple(bottom_in[c, j] for j in range(nj)))

    row_of = lax.broadcasted_iota(jnp.int32, (8, LANES), 0)

    def state_sums(terms):
        if nj != 8 or ns % 8:
            return jnp.concatenate([jnp.sum(term, axis=0, keepdims=True) for term in terms], axis=0)
        level = [sum(term[k:k + 8] for k in range(0, ns, 8)) for term in terms]
        for reach in (1, 2, 4):
            even = (row_of & reach) == 0
            level = [jnp.where(even, first, second)
                     + pltpu.roll(jnp.where(even, second, first), 8 - reach, 0)
                     for first, second in zip(level[0::2], level[1::2])]
        return level[0]

    def gradients(c):
        rates = rates_ref[:, lanes(c)]

        def body(i, state):
            carry = right_in[c, i]
            state = list(state)
            drive_terms, step_terms = [None] * nj, [None] * nj
            for j in reversed(range(nj)):
                a, here, r = decay[c, i, j], cct[c, i, j], rst[c, i, j]
                before = rst[c, i, j - 1] if j else left_in[c, i]
                kept = a * state[j]
                state[j] = kept + r
                row_cot = here + carry
                carry = a * row_cot
                change = here * kept + carry * before
                acc_out[i, j] += gy[c, i, pl.ds(j, 1), :] * state[j]
                acc_in[i, j] += dr[c, i, pl.ds(j, 1), :] * row_cot
                drive_terms[j] = row_cot * im[i, j]
                step_terms[j] = change * rates
            dc_rows[i] = state_sums(drive_terms)
            ds_rows[i] = state_sums(step_terms)
            return tuple(state)

        down_rows(body, tuple(top_in[c, j] for j in range(nj)))
        step = steps_ref[:, lanes(c)].reshape(ni, nj, LANES)
        xf = x_ref[:, lanes(c)].astype(F32).reshape(ni, nj, LANES)
        drive_cot = dc_rows[...] * mb[...]
        gx_ref[:, lanes(c)] = (drive_cot * step).reshape(patches, LANES).astype(jnp.bfloat16)
        gs_ref[:, lanes(c)] = (drive_cot * xf + kb[...] * ds_rows[...]).reshape(patches, LANES)

    @pl.loop(0, chunks)
    def _(c):
        prepare(c)
        open_ends(c)
        send_first(UP, c)
        send_first(RIGHT, c)

    @pl.loop(0, chunks)
    def _(c):
        relay(UP, c)

    acc_in[...] = jnp.zeros_like(acc_in)
    acc_out[...] = jnp.zeros_like(acc_out)

    def do_forward(c):
        relay(RIGHT, c)
        take_last(RIGHT, c)
        forward(c)
        send_first(DOWN, c)

    def do_backward(c):
        take_last(UP, c)
        backward(c)
        send_first(LEFT, c)

    upper = row < rows // 2

    @pl.loop(0, chunks)
    def _(c):
        @pl.when(upper)
        def _():
            do_forward(c)
            do_backward(c)

        @pl.when(jnp.logical_not(upper))
        def _():
            do_backward(c)
            do_forward(c)

        @pl.when(c > 0)
        def _():
            relay(DOWN, c - 1)

    relay(DOWN, chunks - 1)

    @pl.loop(0, chunks)
    def _(c):
        take_last(DOWN, c)
        relay(LEFT, c)
        take_last(LEFT, c)
        gradients(c)

    ones = jnp.ones((8, LANES), jnp.bfloat16)

    def lane_sums(acc):
        whole = acc[...].reshape(patches * ns, LANES)
        high = whole.astype(jnp.bfloat16)
        low = (whole - high.astype(F32)).astype(jnp.bfloat16)

        def dot(part):
            return lax.dot_general(ones, part, (((1,), (1,)), ((), ())), preferred_element_type=F32)

        return dot(high) + dot(low)

    for which, acc in enumerate((acc_in, acc_out)):
        flat = lane_sums(acc)
        for i in range(ni):
            mine[which, pl.ds(i, 1), :] = flat[0:1, i * nj * ns:(i + 1) * nj * ns]
    swap = pltpu.make_async_remote_copy(
        src_ref=mine, dst_ref=theirs, send_sem=pair_send, recv_sem=pair_recv,
        device_id={"chan": peer}, device_id_type=pl.DeviceIdType.MESH)
    swap.start()
    for kind in (RIGHT, UP, DOWN, LEFT):
        if several[kind]:
            @pl.when(jnp.logical_not(sink_edge[kind]))
            def _():
                @pl.loop(0, chunks)
                def _(c):
                    copy(kind, c).wait_send()
    swap.wait()
    for which, target in enumerate((gi_ref, go_ref)):
        total = mine[which] + theirs[which]
        for j in range(nj):
            target[:, j, :] = total[:, j * ns:(j + 1) * ns]


def finish(*refs):
    arrays = (len(refs) - 2) // 3
    sources, targets, held = refs[:arrays], refs[arrays:2 * arrays], refs[2 * arrays:3 * arrays]
    load_sem, store_sem = refs[3 * arrays:]
    loads = [pltpu.make_async_copy(sources[k], held[k], load_sem.at[k]) for k in range(arrays)]
    stores = [pltpu.make_async_copy(held[k], targets[k], store_sem.at[k]) for k in range(arrays)]
    for load in loads:
        load.start()
    for load, store in zip(loads, stores):
        load.wait()
        store.start()
    for store in stores:
        store.wait()


def local(sizes, patches, steps, decay_codes, tissue_mask, decay_rates, input_map, output_map, out_grad):
    rows, cols, chans = sizes
    ni, nj, width = steps.shape
    ns = decay_rates.shape[0]
    chunks = width // LANES
    count = ni * nj
    vmem = pl.BlockSpec(memory_space=pltpu.VMEM)
    hbm = pl.BlockSpec(memory_space=pltpu.HBM)

    def buf(*shape):
        return pltpu.VMEM(shape, F32)

    across = buf(chunks, ni, ns, LANES)
    along = buf(chunks, nj, ns, LANES)
    whole = buf(chunks, ni, nj, ns, LANES)
    tile = buf(ni, nj, LANES)
    tiles = buf(chunks, ni, nj, LANES)
    maps = buf(ni, nj, ns, LANES)
    results = pl.pallas_call(
        functools.partial(kernel, (rows, cols, chans, ni, nj, ns, chunks)),
        out_shape=(
            jax.ShapeDtypeStruct((count, width), jnp.bfloat16),
            jax.ShapeDtypeStruct((count, width), F32),
            jax.ShapeDtypeStruct((ni, nj, ns), F32),
            jax.ShapeDtypeStruct((ni, nj, ns), F32),
        ),
        in_specs=[hbm] * 8,
        out_specs=(vmem,) * 4,
        scratch_shapes=[
            pltpu.VMEM((count, width), jnp.bfloat16), buf(count, width), pltpu.VMEM((nj, ni), jnp.int32),
            pltpu.VMEM((nj, ni), jnp.int32), buf(ns, width), buf(count, ns), buf(count, ns),
            pltpu.VMEM((count, width), jnp.bfloat16), pltpu.SemaphoreType.DMA((8,)),
            maps, maps, tile, tile, tiles, tiles, tiles, buf(chunks, nj, LANES), whole, whole, whole,
            across, across, along, along, along, along, across, across,
            maps, maps, tile, tile, buf(2, ni, nj * ns), buf(2, ni, nj * ns),
            pltpu.SemaphoreType.DMA((4, chunks)), pltpu.SemaphoreType.DMA((4, chunks)),
            pltpu.SemaphoreType.DMA, pltpu.SemaphoreType.DMA,
        ],
        compiler_params=pltpu.CompilerParams(
            collective_id=0, has_side_effects=True, vmem_limit_bytes=63 * 1024 * 1024),
        cost_estimate=pl.CostEstimate(
            flops=40 * count * ns * width, bytes_accessed=16 * count * width,
            transcendentals=count * ns * width),
    )(patches.reshape(count, width), steps.reshape(count, width), decay_codes.T, tissue_mask.T, decay_rates,
      input_map.reshape(count, ns), output_map.reshape(count, ns), out_grad.reshape(count, width))
    gx, gs, gi, go = pl.pallas_call(
        finish,
        out_shape=tuple(jax.ShapeDtypeStruct(value.shape, value.dtype) for value in results),
        in_specs=[hbm] * 4,
        out_specs=(hbm,) * 4,
        scratch_shapes=[pltpu.VMEM(value.shape, value.dtype) for value in results]
        + [pltpu.SemaphoreType.DMA((4,))] * 2,
        compiler_params=pltpu.CompilerParams(vmem_limit_bytes=63 * 1024 * 1024),
    )(*results)
    shape = (ni, nj, width)
    return gx.reshape(shape), gs.reshape(shape), gi, go


def solution(mesh):
    field = P(("groups", "rows"), "cols", "chan")
    plain = P(("groups", "rows"), "cols")
    proj = P(("groups", "rows"), "cols", None)
    sizes = (mesh.shape["rows"], mesh.shape["cols"], mesh.shape["chan"])
    return jax.shard_map(
        functools.partial(local, sizes), mesh=mesh,
        in_specs=(field, field, plain, plain, P(None, "chan"), proj, proj, field),
        out_specs=(field, field, proj, proj), check_vma=False)
```
